256 devices in a mesh: bl: 32 (over x, y, core), lst: 8 (over z).
Axes of the slice: x: 4, y: 4, z: 8, core: 2. Of those that a mesh axis runs over, the one named last changes fastest.
Arguments:
- visibility: bfloat16 [1024, 128, 2, 1536], P('bl', 'lst'), may hold values from -6 to 6
- channel_flags: int32 [128, 1536], P('lst'), may hold values 0 or 1
- time_bins: int32 [128], P('lst'), may hold values from 0 to 15
- baseline_group_index: int32 [1024], replicated, may hold values from 0 to 63, as said below
- owner_map: int32 [64], replicated, may hold values from 0 to 63, as said below
Outputs:
- delay_power: float32 [64, 16, 1536], P('bl', 'lst')
The draws below stay inside these ranges and needn't reach their ends.
Inputs may be any that keep to these rules, and one draw needn't show every extreme that they name: `baseline_group_index`: every group holds 2 or more baselines. Of the 32 baselines of one index of bl, at most 2 lie in groups of one owner, the owner of group g being owner_map[g] // 2; some index of bl has exactly 2 for some owner, and some owner receives exactly 2 from every index of bl. `owner_map`: A permutation of the groups.
All inputs are finite; a program needn't handle non-finite values. No bound on the sum of `channel_flags` on one device may be relied on, other than what follows from the above.
Results may differ from the reference program's by a relative error of at most 0.0068.
Values may be sent and summed in bfloat16 or wider, within the bound.
A program may use at most 128 MiB of HBM per device.

```python
import math
import jax
import jax.numpy as jnp
from jax import lax

F = 1536
BL_DEV = 32
GROUPS_DEV = 2
CAP = 2
BL = 1024
TIMES = 128
GROUPS = 64
BINS = 16
N_BL = 32


def baseline_rows(key):
    streams = jax.random.split(key, 6)
    devices = jnp.arange(N_BL, dtype=jnp.int32)
    start_offset = jax.random.randint(streams[0], (), 1, N_BL).astype(jnp.int32)
    heaviest = jax.random.randint(streams[1], (), 0, N_BL).astype(jnp.int32)
    leading = devices
    trailing = (devices + start_offset) % N_BL
    has_extra = (heaviest != leading) & (heaviest != trailing)
    extra = jnp.full((N_BL,), heaviest, jnp.int32)
    owners = jnp.arange(N_BL, dtype=jnp.int32)
    taken = CAP * ((owners[None, :] == leading[:, None]).astype(jnp.int32) + (owners[None, :] == trailing[:, None]).astype(jnp.int32) + ((owners[None, :] == extra[:, None]) & has_extra[:, None]).astype(jnp.int32))
    cand_owner = jnp.repeat(owners, CAP)
    cand_copy = jnp.tile(jnp.arange(CAP, dtype=jnp.int32), N_BL)
    allowed = cand_copy[None, :] < CAP - taken[:, cand_owner]
    position = jnp.arange(N_BL * CAP, dtype=jnp.int32)
    scores = jax.random.randint(streams[2], (N_BL, N_BL * CAP), 0, 2 ** 20) * (N_BL * CAP) + position[None, :]
    scores = jnp.where(allowed, scores, -1 - position[None, :])
    ranking = jnp.argsort(-scores, axis=1)
    picked = cand_owner[ranking]
    column = jnp.arange(BL_DEV, dtype=jnp.int32)[None, :]
    start = jnp.where(has_extra, 3 * CAP, 2 * CAP)[:, None]
    pick_index = jnp.clip(column - start, 0, N_BL * CAP - 1)
    later = jnp.take_along_axis(picked, pick_index, axis=1)
    owner_of = jnp.where(column < CAP, leading[:, None], jnp.where(column < 2 * CAP, trailing[:, None], jnp.where(column < start, extra[:, None], later)))
    spread = jax.random.randint(streams[3], (N_BL, BL_DEV), 0, GROUPS_DEV).astype(jnp.int32)
    local_group = jnp.where(column < CAP, 0, jnp.where(column < 2 * CAP, GROUPS_DEV - 1, spread))
    row_of = owner_of * GROUPS_DEV + local_group
    shuffle = jnp.argsort(jax.random.randint(streams[4], (N_BL, BL_DEV), 0, 2 ** 20) * BL_DEV + column, axis=1)
    row_of = jnp.take_along_axis(row_of, shuffle, axis=1).reshape(-1)
    labels = jax.random.permutation(streams[5], GROUPS).astype(jnp.int32)
    inverse = jnp.argsort(labels).astype(jnp.int32)
    return (inverse[row_of].astype(jnp.int32), labels)


def draw_baseline_group_index(key, part):
    shared = baseline_rows(key)
    return shared[0]


def draw_owner_map(key, part):
    shared = baseline_rows(key)
    return shared[1]


def set_ends(entries, rng, low, high):
    shape = entries.shape
    spot = [jax.random.randint(jax.random.fold_in(rng, axis), (), 0, shape[axis]) for axis in range(len(shape))]
    entries = entries.at[tuple(spot)].set(low)
    longest = shape.index(max(shape))
    spot[longest] = (spot[longest] + 1) % shape[longest]
    return entries.at[tuple(spot)].set(high)


def level_of(stream_key, shape, cuts, smallest, largest):
    factor_of, own = 1.0, jax.random.fold_in(stream_key, 6)
    for axis_at, blocks in cuts:
        heights = jnp.exp(jax.random.uniform(jax.random.fold_in(own, axis_at), (blocks,), jnp.float32, smallest / len(cuts), largest / len(cuts)))
        factor_of = factor_of * jnp.repeat(heights, shape[axis_at] // blocks).reshape([-1 if axis == axis_at else 1 for axis in range(len(shape))])
    return factor_of


def scatter_about(own_key, shape, scale, reach, pieces=(), kind=jnp.bfloat16):
    result = jax.random.normal(own_key, shape, jnp.float32) * scale
    if len(pieces) > 0:
        result = level_of(own_key, shape, pieces, -0.22, 0.18) * result
    return jnp.clip(result, min=-reach, max=reach).astype(kind)


def setup_inputs(seed: int = 0) -> dict:
    arg_keys = jax.random.split(jax.random.key(seed), 6)
    return {
        "visibility": scatter_about(arg_keys[0], (BL, TIMES, 2, F), 1.0, 6.0, ((0, 32), (1, 8))),
        "channel_flags": set_ends((jax.random.randint(arg_keys[1], (TIMES, F), 0, 8) < 7).astype(jnp.int32), jax.random.fold_in(arg_keys[1], 1), 0, 1),
        "time_bins": set_ends(jax.random.randint(arg_keys[2], (TIMES,), 0, BINS), jax.random.fold_in(arg_keys[2], 1), 0, BINS - 1).astype(jnp.int32),
        "baseline_group_index": draw_baseline_group_index(jax.random.fold_in(arg_keys[5], 71), 0),
        "owner_map": draw_owner_map(jax.random.fold_in(arg_keys[5], 71), 0),
    }


def taper_weights(channel_flags, channels):
    channel_axis = jnp.arange(channels, dtype=jnp.int32).astype(jnp.float32)
    phase = channel_axis * (2.0 * math.pi / channels)
    taper = 0.35875 - 0.48829 * jnp.cos(phase) + 0.14128 * jnp.cos(2.0 * phase) - 0.01168 * jnp.cos(3.0 * phase)
    return taper[None, :] * channel_flags.astype(jnp.float32)

def dft_tables(channels):
    counter = jnp.arange(channels, dtype=jnp.int32)
    product = counter[:, None] * counter[None, :] % channels
    angle = product.astype(jnp.float32) * (2.0 * math.pi / channels)
    factor = 1.0 / math.sqrt(channels)
    return ((jnp.cos(angle) * factor).astype(jnp.bfloat16), (jnp.sin(angle) * factor).astype(jnp.bfloat16))

def transform(samples, weights, cos_table, sin_table):
    baseline_total_count, time_count, _, channels = samples.shape
    tapered = (samples.astype(jnp.float32) * weights[None, :, None, :]).astype(jnp.bfloat16)
    flat = tapered.reshape(-1, channels)
    along_cos = jnp.dot(flat, cos_table, preferred_element_type=jnp.float32).reshape(baseline_total_count, time_count, 2, channels)
    along_sin = jnp.dot(flat, sin_table, preferred_element_type=jnp.float32).reshape(baseline_total_count, time_count, 2, channels)
    real_part = along_cos[:, :, 0] + along_sin[:, :, 1]
    imag_part = along_cos[:, :, 1] - along_sin[:, :, 0]
    return jnp.stack([real_part, imag_part], axis=2).astype(jnp.bfloat16)

def reference(visibility, channel_flags, time_bins, baseline_group_index, owner_map):
    weights = taper_weights(channel_flags, F)
    cos_table, sin_table = dft_tables(F)
    blocks = visibility.reshape(N_BL, BL_DEV, TIMES, 2, F)
    spectra = lax.map(lambda block: transform(block, weights, cos_table, sin_table), blocks).reshape(BL, TIMES, 2, F)
    rows = owner_map[baseline_group_index]
    widened = spectra.astype(jnp.float32)
    summed = jax.ops.segment_sum(widened, rows, num_segments=GROUPS)
    squares = jax.ops.segment_sum(widened[:, :, 0] * widened[:, :, 0] + widened[:, :, 1] * widened[:, :, 1], rows, num_segments=GROUPS)
    counts = jax.ops.segment_sum(jnp.ones((BL,), jnp.float32), rows, num_segments=GROUPS)
    inverse_pairs = 1.0 / (counts * (counts - 1.0))
    cross = (summed[:, :, 0] * summed[:, :, 0] + summed[:, :, 1] * summed[:, :, 1] - squares) * inverse_pairs[:, None, None]
    bin_table = (time_bins[:, None] == jnp.arange(BINS, dtype=jnp.int32)[None, :]).astype(jnp.float32)
    return jnp.einsum('qtk,tj->qjk', cross, bin_table, precision=lax.Precision.HIGHEST)
```

```python
import functools
import math

import jax
import jax.numpy as jnp
import numpy as np
from jax import lax
from jax.experimental import pallas as pl
from jax.experimental.pallas import tpu as pltpu
from jax.sharding import PartitionSpec as P

MESH = pl.DeviceIdType.MESH
F = 1536
H = F // 2
NC = 3
NB = 32
PIECES = 4
PB = NB // PIECES
BF = jnp.bfloat16
F32 = jnp.float32


def tables():
    f = np.arange(H, dtype=np.int64)[:, None]
    m = np.arange(H // 2, dtype=np.int64)[None, :]
    out = np.zeros((2, H, NC, 2, 128), np.float32)
    for parity in range(2):
        k = 2 * m + parity
        angle = 2.0 * np.pi * ((f * k) % F) / F
        cos, sin = np.cos(angle), np.sin(angle)
        if parity == 0:
            sin[:, 0] = np.cos(np.pi * f[:, 0])
        out[parity, :, :, 0] = (cos / math.sqrt(F)).reshape(H, NC, 128)
        out[parity, :, :, 1] = (sin / math.sqrt(F)).reshape(H, NC, 128)
    return out.reshape(2, H, NC * 256).astype(jnp.bfloat16)


def taper_row():
    phase = np.arange(F, dtype=np.float32) * np.float32(2.0 * math.pi / F)
    phase = phase.astype(np.float64)
    taper = (
        0.35875
        - 0.48829 * np.cos(phase)
        + 0.14128 * np.cos(2.0 * phase)
        - 0.01168 * np.cos(3.0 * phase)
    )
    return taper.astype(np.float32)[None, :]


def kernel(
    idx_ref, inv_ref, vis_ref, tab_hbm, flags_ref, taper_ref, bins_ref,
    out_ref,
    xv, w2, yall, ysend, tab, ra, rb, planes, send1, recv1, send2, recv2, power, zsend, zrecv,
    ld_sem, tab_sem, ys_sem, yr_sem, s1_sem, r1_sem, s2_sem, r2_sem, zs_sem, zr_sem,
):
    bl = lax.axis_index("bl")
    z = lax.axis_index("lst")
    c = lax.rem(bl, 2)
    y = lax.rem(bl // 2, 4)
    x = bl // 8

    def at(xx, yy, cc, zz):
        return (xx * 8 + yy * 2 + cc, zz)

    def x_peer(d):
        return at(lax.rem(x + d, 4), y, c, z)

    def y_peer(d):
        return at(x, lax.rem(y + d, 4), c, z)

    def z_peer(d, e):
        return at(x, y, lax.rem(c + e, 2), lax.rem(z + d, 8))

    z_offsets = [(d, e) for d in range(8) for e in range(2) if d or e]

    rows = vis_ref.reshape(NB, 32, F)
    loads = []
    for p in range(PIECES):
        cp = pltpu.make_async_copy(
            rows.at[pl.ds(p * PB, PB)], xv.at[pl.ds(p * PB, PB)], ld_sem.at[p]
        )
        cp.start()
        loads.append(cp)
    tab_cp = pltpu.make_async_copy(tab_hbm.at[c], tab, tab_sem)
    tab_cp.start()

    barrier = pltpu.get_barrier_semaphore()
    peers = [z_peer(d, e) for d, e in z_offsets]
    peers += [x_peer(d) for d in (1, 2, 3)] + [y_peer(d) for d in (1, 2, 3)]
    for peer in peers:
        pl.semaphore_signal(barrier, inc=1, device_id=peer, device_id_type=MESH)

    for t in range(16):
        row = taper_ref[...] * flags_ref[pl.ds(t, 1), :].astype(F32)
        w2[pl.ds(2 * t, 2), :] = jnp.broadcast_to(row, (2, F))
    planes[2 * NB] = jnp.zeros((6, 16, 128), F32)
    sign = (1 - 2 * c).astype(F32)

    pl.semaphore_wait(barrier, len(peers))
    exchange = []
    for p in range(PIECES):
        loads[p].wait()

        def fold(b, carry):
            for j in range(6):
                lo_at, hi_at = pl.ds(j * 128, 128), pl.ds(H + j * 128, 128)
                lo = (xv[b, :, lo_at].astype(F32) * w2[:, lo_at]).astype(BF).astype(F32)
                hi = (xv[b, :, hi_at].astype(F32) * w2[:, hi_at]).astype(BF).astype(F32)
                hi = hi * sign
                at_rows = pl.ds(pl.multiple_of(b * 32, 32), 32)
                yall[0, at_rows, lo_at] = (lo + hi).astype(BF)
                ysend[at_rows, lo_at] = (lo - hi).astype(BF)
            return carry

        lax.fori_loop(p * PB, (p + 1) * PB, fold, 0)
        piece = pl.ds(p * PB * 32, PB * 32)
        cp = pltpu.make_async_remote_copy(
            src_ref=ysend.at[piece],
            dst_ref=yall.at[1, piece],
            send_sem=ys_sem.at[p],
            recv_sem=yr_sem.at[p],
            device_id=z_peer(0, 1),
            device_id_type=MESH,
        )
        cp.start()
        exchange.append(cp)
    tab_cp.wait()

    def first(half, n, d):
        peer = x_peer(d) if half == 0 else y_peer(d)
        mine = x if half == 0 else y
        return pltpu.make_async_remote_copy(
            src_ref=send1.at[half, n, lax.rem(mine + d, 4)],
            dst_ref=recv1.at[half, n, d - 1],
            send_sem=s1_sem.at[half, n, d - 1],
            recv_sem=r1_sem.at[half, n, d - 1],
            device_id=peer,
            device_id_type=MESH,
        )

    def second(half, n, d):
        peer = y_peer(d) if half == 0 else x_peer(d)
        mine = y if half == 0 else x
        return pltpu.make_async_remote_copy(
            src_ref=send2.at[half, n, lax.rem(mine + d, 4)],
            dst_ref=recv2.at[half, n, d - 1],
            send_sem=s2_sem.at[half, n, d - 1],
            recv_sem=r2_sem.at[half, n, d - 1],
            device_id=peer,
            device_id_type=MESH,
        )

    lane = lax.broadcasted_iota(jnp.int32, (1, 128), 1)
    for n in range(NC):
        special = (lane + c) == 0
        for side in range(2):
            if side == 1 and n == 0:
                for cp in exchange:
                    cp.wait_recv()

            def transform(i, carry):
                at_rows = pl.ds(pl.multiple_of(i * 512, 512), 512)
                prod = jnp.dot(
                    yall[side, at_rows, :],
                    tab[:, pl.ds(n * 256, 256)],
                    preferred_element_type=F32,
                )
                ra[...] = prod[:, :128]
                rb[...] = prod[:, 128:]

                def split(b, carry):
                    start = b * 32
                    ar = ra[pl.ds(start, 16, stride=2), :]
                    ai = ra[pl.ds(start + 1, 16, stride=2), :]
                    br = rb[pl.ds(start, 16, stride=2), :]
                    bi = rb[pl.ds(start + 1, 16, stride=2), :]
                    if n == 0:
                        zero = jnp.zeros_like(ar)
                        pr = ar + jnp.where(special, zero, bi)
                        pi = ai - jnp.where(special, zero, br)
                        mr = jnp.where(special, br, ar - bi)
                        mi = jnp.where(special, bi, ai + br)
                    else:
                        pr, pi, mr, mi = ar + bi, ai - br, ar - bi, ai + br
                    at_b = side * NB + i * 16 + b
                    planes[at_b, 0] = pr
                    planes[at_b, 1] = pi
                    planes[at_b, 2] = pr * pr + pi * pi
                    planes[at_b, 3] = mr
                    planes[at_b, 4] = mi
                    planes[at_b, 5] = mr * mr + mi * mi
                    return carry

                return lax.fori_loop(0, 16, split, carry)

            lax.fori_loop(0, 2, transform, 0)

        def gather(q, carry):
            members = [idx_ref[q, s] for s in range(4)]
            qx, qy, qg = q // 16, lax.rem(q // 4, 4), lax.rem(q, 4)
            for plane in range(6):
                total = planes[members[0], plane] + planes[members[1], plane]
                total += planes[members[2], plane] + planes[members[3], plane]
                total = total.astype(BF)
                if plane < 3:
                    send1[0, n, qx, qy * 4 + qg, plane] = total
                else:
                    send1[1, n, qy, qx * 4 + qg, plane - 3] = total
            return carry

        lax.fori_loop(0, 64, gather, 0)
        for d in (2, 1, 3):
            for half in range(2):
                first(half, n, d).start()

    for n in range(NC):
        for half in range(2):
            for d in (1, 2, 3):
                first(half, n, d).wait_recv()
            mine = x if half == 0 else y

            def combine(i, carry):
                total = send1[half, n, mine, i].astype(F32)
                for d in (1, 2, 3):
                    total += recv1[half, n, d - 1, i].astype(F32)
                send2[half, n, i // 4, lax.rem(i, 4)] = total.astype(BF)
                return carry

            lax.fori_loop(0, 16, combine, 0)
            for d in (2, 1, 3):
                second(half, n, d).start()

    for n in range(NC):
        for half in range(2):
            for d in (1, 2, 3):
                second(half, n, d).wait_recv()
            mine = y if half == 0 else x

            def finish(g, carry):
                total = send2[half, n, mine, g].astype(F32)
                for d in (1, 2, 3):
                    total += recv2[half, n, d - 1, g].astype(F32)
                at_rows = pl.ds(pl.multiple_of(half * 64 + g * 16, 16), 16)
                power[at_rows, :] = total[0] * total[0] + total[1] * total[1] - total[2]
                return carry

            lax.fori_loop(0, 4, finish, 0)
        value = power[...]
        high = value.astype(BF)
        low = (value - high.astype(F32)).astype(BF)
        onehot = bins_ref[...]
        binned = jnp.dot(onehot, high, preferred_element_type=F32)
        binned += jnp.dot(onehot, low, preferred_element_type=F32)
        zsend[:, :, pl.ds(n * 128, 128)] = binned.reshape(16, 8, 128)

    me = z * 2 + c
    spread = []
    for i, (d, e) in enumerate(z_offsets):
        dest = lax.rem(z + d, 8) * 2 + lax.rem(c + e, 2)
        cp = pltpu.make_async_remote_copy(
            src_ref=zsend.at[dest],
            dst_ref=zrecv.at[c, d],
            send_sem=zs_sem.at[i],
            recv_sem=zr_sem.at[i],
            device_id=z_peer(d, e),
            device_id_type=MESH,
        )
        cp.start()
        spread.append(cp)
    zrecv[c, 0] = zsend[me]
    for cp in spread:
        cp.wait_recv()

    parts = []
    for parity in range(2):
        total = zrecv[parity, 0]
        for d in range(1, 8):
            total += zrecv[parity, d]
        parts.append(total)
    even, odd = parts
    row = lax.broadcasted_iota(jnp.int32, (256, 256), 0)
    col = lax.broadcasted_iota(jnp.int32, (256, 256), 1)
    step = col // 2
    from_even = lax.rem(col, 2) == 0
    up = (row == jnp.where(from_even, step, 128 + step)).astype(BF)
    down = (row == jnp.where(from_even, lax.rem(128 - step, 128), 255 - step)).astype(BF)

    def shuffled(value, perm):
        a = value.astype(BF)
        rest = value - a.astype(F32)
        b = rest.astype(BF)
        cc = (rest - b.astype(F32)).astype(BF)
        out = jnp.dot(a, perm, preferred_element_type=F32)
        out += jnp.dot(b, perm, preferred_element_type=F32)
        return out + jnp.dot(cc, perm, preferred_element_type=F32)

    def cut(value, n):
        return value[:, n * 128 : (n + 1) * 128]

    for n in range(NC):
        plus = shuffled(jnp.concatenate([cut(even, n), cut(odd, n)], axis=1), up)
        even_down = jnp.where(lane == 0, cut(even, (3 - n) % 3), cut(even, 2 - n))
        minus = shuffled(jnp.concatenate([even_down, cut(odd, 2 - n)], axis=1), down)
        for g in range(2):
            out_ref[g, :, pl.ds(n * 256, 256)] = plus[2 * g : 2 * g + 2] * inv_ref[g]
            out_ref[g, :, pl.ds(H + n * 256, 256)] = minus[4 + 2 * g : 6 + 2 * g] * inv_ref[g]

    for cp in exchange + spread:
        cp.wait_send()
    for n in range(NC):
        for half in range(2):
            for d in (1, 2, 3):
                first(half, n, d).wait_send()
                second(half, n, d).wait_send()


def on_device(visibility, channel_flags, time_bins, baseline_group_index, owner_map):
    bl = lax.axis_index("bl")
    chip, core = bl // 2, bl % 2
    groups = jnp.arange(64, dtype=jnp.int32)
    own = lax.dynamic_slice_in_dim(baseline_group_index, bl * NB, NB)
    other = lax.dynamic_slice_in_dim(baseline_group_index, (chip * 2 + 1 - core) * NB, NB)
    local = jnp.concatenate([own, other])
    row_of = (owner_map[None, :] == groups[:, None]).astype(F32)
    group_of = (local[None, :] == groups[:, None]).astype(F32)
    member = jnp.dot(row_of, group_of, preferred_element_type=F32)
    before = (groups[:, None] < groups[None, :]).astype(F32)
    rank = jnp.dot(member, before, preferred_element_type=F32)
    slots = jnp.arange(4, dtype=jnp.int32).astype(F32)
    chosen = member[:, None, :] * (rank[:, None, :] == slots[None, :, None]).astype(F32)
    offset = jnp.sum(chosen * (64 - groups).astype(F32)[None, None, :], axis=2)
    idx = (64.0 - offset).astype(jnp.int32)
    totals = jnp.sum(
        (baseline_group_index[None, :] == groups[:, None]).astype(F32), axis=1
    )
    mine = bl * 2 + jnp.arange(2, dtype=jnp.int32)
    count = jnp.sum((owner_map[None, :] == mine[:, None]).astype(F32) * totals[None, :], axis=1)
    inverse = 1.0 / (count * (count - 1.0))

    r = jnp.arange(128, dtype=jnp.int32)
    r_bin = (r // 16) * 2 + r % 2
    r_half, r_group = (r // 4) % 2, ((r // 8) % 2) * 2 + (r // 2) % 2
    k_half, k_group = r // 64, (r // 16) % 4
    k_bin = jnp.tile(time_bins, 8)
    bins = (
        (r_bin[:, None] == k_bin[None, :])
        & (r_half[:, None] == k_half[None, :])
        & (r_group[:, None] == k_group[None, :])
    ).astype(BF)

    tab = jnp.asarray(tables())
    taper = jnp.asarray(taper_row())
    smem = pl.BlockSpec(memory_space=pltpu.SMEM)
    vmem = pl.BlockSpec(memory_space=pltpu.VMEM)
    anym = pl.BlockSpec(memory_space=pl.ANY)
    dma = pltpu.SemaphoreType.DMA
    return pl.pallas_call(
        kernel,
        out_shape=jax.ShapeDtypeStruct((2, 2, F), F32),
        in_specs=[smem, smem, anym, anym, vmem, vmem, vmem],
        out_specs=vmem,
        scratch_shapes=[
            pltpu.VMEM((NB, 32, F), BF),
            pltpu.VMEM((32, F), F32),
            pltpu.VMEM((2, NB * 32, H), BF),
            pltpu.VMEM((NB * 32, H), BF),
            pltpu.VMEM((H, NC * 256), BF),
            pltpu.VMEM((512, 128), F32),
            pltpu.VMEM((512, 128), F32),
            pltpu.VMEM((2 * NB + 1, 6, 16, 128), F32),
            pltpu.VMEM((2, NC, 4, 16, 3, 16, 128), BF),
            pltpu.VMEM((2, NC, 3, 16, 3, 16, 128), BF),
            pltpu.VMEM((2, NC, 4, 4, 3, 16, 128), BF),
            pltpu.VMEM((2, NC, 3, 4, 3, 16, 128), BF),
            pltpu.VMEM((128, 128), F32),
            pltpu.VMEM((16, 8, NC * 128), F32),
            pltpu.VMEM((2, 8, 8, NC * 128), F32),
            dma((PIECES,)),
            dma,
            dma((PIECES,)),
            dma((PIECES,)),
            dma((2, NC, 3)),
            dma((2, NC, 3)),
            dma((2, NC, 3)),
            dma((2, NC, 3)),
            dma((15,)),
            dma((15,)),
        ],
        compiler_params=pltpu.CompilerParams(
            collective_id=0, has_side_effects=True, vmem_limit_bytes=56 << 20
        ),
        name="spectra_power",
    )(idx, inverse, visibility, tab, channel_flags, taper, bins)


def solution(mesh):
    in_specs = (P("bl", "lst", None, None), P("lst", None), P("lst"), P(), P())
    out_specs = P("bl", "lst", None)
    return jax.shard_map(
        on_device, mesh=mesh, in_specs=in_specs, out_specs=out_specs, check_vma=False
    )
```

```python
import functools
import math

import jax
import jax.numpy as jnp
import numpy as np
from jax import lax
from jax.experimental import pallas as pl
from jax.experimental.pallas import tpu as pltpu
from jax.sharding import PartitionSpec as P

MESH = pl.DeviceIdType.MESH
F = 1536
H = F // 2
NC = 3
NB = 32
PIECES = 4
PB = NB // PIECES
BF = jnp.bfloat16
F32 = jnp.float32


def tables():
    f = np.arange(H, dtype=np.int64)[:, None]
    m = np.arange(H // 2, dtype=np.int64)[None, :]
    out = np.zeros((2, H, NC, 2, 128), np.float32)
    for parity in range(2):
        k = 2 * m + parity
        angle = 2.0 * np.pi * ((f * k) % F) / F
        cos, sin = np.cos(angle), np.sin(angle)
        if parity == 0:
            sin[:, 0] = np.cos(np.pi * f[:, 0])
        out[parity, :, :, 0] = (cos / math.sqrt(F)).reshape(H, NC, 128)
        out[parity, :, :, 1] = (sin / math.sqrt(F)).reshape(H, NC, 128)
    return out.reshape(2, H, NC * 256).astype(jnp.bfloat16)


def taper_row():
    phase = np.arange(F, dtype=np.float32) * np.float32(2.0 * math.pi / F)
    phase = phase.astype(np.float64)
    taper = (
        0.35875
        - 0.48829 * np.cos(phase)
        + 0.14128 * np.cos(2.0 * phase)
        - 0.01168 * np.cos(3.0 * phase)
    )
    return taper.astype(np.float32)[None, :]


def kernel(
    vis_ref, tab_hbm, flags_ref, taper_ref, times_ref, group_ref, owner_ref,
    out_ref,
    idx_v, idx_ref, bins_ref, inv_ref,
    xv, w2, yall, ysend, tab, ra, rb, planes, send1, recvf, recv1, send2, recv2,
    power, zsend, zrecv,
    ld_sem, tab_sem, idx_sem, ys_sem, yr_sem, s1_sem, r1_sem, s2_sem, r2_sem,
    zs_sem, zr_sem,
):
    bl = lax.axis_index("bl")
    z = lax.axis_index("lst")
    c = lax.rem(bl, 2)
    y = lax.rem(bl // 2, 4)
    x = bl // 8

    def at(xx, yy, cc, zz):
        return (xx * 8 + yy * 2 + cc, zz)

    def x_peer(d):
        return at(lax.rem(x + d, 4), y, c, z)

    def y_peer(d):
        return at(x, lax.rem(y + d, 4), c, z)

    def z_peer(d, e):
        return at(x, y, lax.rem(c + e, 2), lax.rem(z + d, 8))

    z_offsets = [(d, e) for d in range(8) for e in range(2) if d or e]

    rows = vis_ref.reshape(NB, 32, F)
    loads = []
    for p in range(PIECES):
        cp = pltpu.make_async_copy(
            rows.at[pl.ds(p * PB, PB)], xv.at[pl.ds(p * PB, PB)], ld_sem.at[p]
        )
        cp.start()
        loads.append(cp)
    tab_cp = pltpu.make_async_copy(tab_hbm.at[c], tab, tab_sem)
    tab_cp.start()

    barrier = pltpu.get_barrier_semaphore()
    peers = [z_peer(d, e) for d, e in z_offsets]
    peers += [x_peer(d) for d in (1, 2, 3)] + [y_peer(d) for d in (1, 2, 3)]
    for peer in peers:
        pl.semaphore_signal(barrier, inc=1, device_id=peer, device_id_type=MESH)

    for t in range(16):
        row = taper_ref[...] * flags_ref[pl.ds(t, 1), :].astype(F32)
        w2[pl.ds(2 * t, 2), :] = jnp.broadcast_to(row, (2, F))
    planes[2 * NB] = jnp.zeros((6, 16, 128), F32)
    sign = (1 - 2 * c).astype(F32)

    pl.semaphore_wait(barrier, len(peers))
    exchange = []
    for p in range(PIECES):
        loads[p].wait()

        def fold(b, carry):
            for j in range(6):
                lo_at, hi_at = pl.ds(j * 128, 128), pl.ds(H + j * 128, 128)
                lo = (xv[b, :, lo_at].astype(F32) * w2[:, lo_at]).astype(BF).astype(F32)
                hi = (xv[b, :, hi_at].astype(F32) * w2[:, hi_at]).astype(BF).astype(F32)
                hi = hi * sign
                at_rows = pl.ds(pl.multiple_of(b * 32, 32), 32)
                yall[0, at_rows, lo_at] = (lo + hi).astype(BF)
                ysend[at_rows, lo_at] = (lo - hi).astype(BF)
            return carry

        lax.fori_loop(p * PB, (p + 1) * PB, fold, 0)
        piece = pl.ds(p * PB * 32, PB * 32)
        cp = pltpu.make_async_remote_copy(
            src_ref=ysend.at[piece],
            dst_ref=yall.at[1, piece],
            send_sem=ys_sem.at[p],
            recv_sem=yr_sem.at[p],
            device_id=z_peer(0, 1),
            device_id_type=MESH,
        )
        cp.start()
        exchange.append(cp)

    def iota(shape, dim):
        return lax.broadcasted_iota(jnp.int32, shape, dim)

    def dot(a, b):
        return jnp.dot(a, b, preferred_element_type=F32)

    def flag(condition):
        return condition.astype(F32).astype(BF)

    chip = bl // 2
    groups = group_ref[pl.ds(chip // 2, 1), :]
    here = iota((64, 128), 1) // 64 == lax.rem(chip, 2)
    group_of = flag((iota((64, 128), 0) == groups) & here)
    row_of = flag(iota((64, 64), 0) == owner_ref[...])
    member = dot(row_of, group_of)
    rank = dot(member.astype(BF), flag(iota((128, 128), 0) < iota((128, 128), 1)))
    place = lax.rem(iota((128, 128), 0) + 32 * c, 64)
    offset = jnp.zeros((64, 128), F32)
    for s in range(4):
        weight = jnp.where(iota((128, 128), 1) == s, 64 - place, 0).astype(F32).astype(BF)
        offset += dot(flag((member > 0.5) & (rank == float(s))), weight)
    idx_v[...] = 64 - offset.astype(jnp.int32)
    idx_cp = pltpu.make_async_copy(idx_v, idx_ref, idx_sem)
    idx_cp.start()

    def late_tables():
        seen = jnp.zeros((64, 128), F32)
        for r in range(8):
            seen += (iota((64, 128), 0) == group_ref[pl.ds(r, 1), :]).astype(F32)
        totals = dot(seen.astype(BF), jnp.ones((128, 128), BF))
        mine8 = 2 * bl + lax.rem(iota((8, 64), 0) // 2, 2)
        count = dot(flag(owner_ref[...] == mine8), totals.astype(BF))
        inv_ref[...] = 1.0 / (count * (count - 1.0))

        times = times_ref[...].astype(F32).astype(BF)
        spread_times = flag(lax.rem(iota((16, 128), 1), 16) == iota((16, 128), 0))
        k_bin = dot(times, spread_times).astype(jnp.int32)
        r, k = iota((128, 128), 0), iota((128, 128), 1)
        bins_ref[...] = flag(
            ((r // 16) * 2 + lax.rem(r, 2) == k_bin)
            & (lax.rem(r // 4, 2) == k // 64)
            & (lax.rem(r // 8, 2) * 2 + lax.rem(r // 2, 2) == lax.rem(k // 16, 4))
        )

    tab_cp.wait()

    def peer1(half, d):
        return x_peer(d) if half == 0 else y_peer(d)

    def peer2(half, d):
        return y_peer(d) if half == 0 else x_peer(d)

    def mine1(half):
        return x if half == 0 else y

    def mine2(half):
        return y if half == 0 else x

    def remote(src, dst, send_sem, recv_sem, device):
        return pltpu.make_async_remote_copy(
            src_ref=src,
            dst_ref=dst,
            send_sem=send_sem,
            recv_sem=recv_sem,
            device_id=device,
            device_id_type=MESH,
        )

    def first(half, n, kind, way):
        d = (1, 3)[way]
        dest = lax.rem(mine1(half) + (2 if kind == 0 else d), 4)
        start = 8 * way if kind != 1 else 8 * (1 - way)
        some = pl.ds(start, 8)
        src = send1.at[half, n, dest, some]
        dst = recvf.at[half, n, way] if kind == 0 else recv1.at[half, n, way, some]
        sems = (s1_sem.at[half, n, kind, way], r1_sem.at[half, n, kind, way])
        return remote(src, dst, *sems, peer1(half, d))

    def second(half, n, d):
        sems = (s2_sem.at[half, n, d - 1], r2_sem.at[half, n, d - 1])
        src = send2.at[half, n, lax.rem(mine2(half) + d, 4)]
        return remote(src, recv2.at[half, n, d - 1], *sems, peer2(half, d))

    def enhance(n):
        for half in range(2):
            for way in range(2):
                first(half, n, 0, way).wait_recv()
                dest = lax.rem(mine1(half) + (1, 3)[way], 4)

                def add(i, carry):
                    at_row = way * 8 + i
                    total = send1[half, n, dest, at_row].astype(F32)
                    total += recvf[half, n, way, i].astype(F32)
                    send1[half, n, dest, at_row] = total.astype(BF)
                    return carry

                lax.fori_loop(0, 8, add, 0, unroll=2)
                first(half, n, 2, way).start()

    lane = lax.broadcasted_iota(jnp.int32, (1, 128), 1)
    for n in range(NC):
        special = (lane + c) == 0
        for side in range(2):
            if side == 1 and n == 0:
                for cp in exchange:
                    cp.wait_recv()

            def transform(i, carry):
                at_rows = pl.ds(pl.multiple_of(i * 512, 512), 512)
                prod = jnp.dot(
                    yall[side, at_rows, :],
                    tab[:, pl.ds(n * 256, 256)],
                    preferred_element_type=F32,
                )
                ra[...] = prod[:, :128]
                rb[...] = prod[:, 128:]

                def split(b, carry):
                    start = b * 32
                    ar = ra[pl.ds(start, 16, stride=2), :]
                    ai = ra[pl.ds(start + 1, 16, stride=2), :]
                    br = rb[pl.ds(start, 16, stride=2), :]
                    bi = rb[pl.ds(start + 1, 16, stride=2), :]
                    if n == 0:
                        zero = jnp.zeros_like(ar)
                        pr = ar + jnp.where(special, zero, bi)
                        pi = ai - jnp.where(special, zero, br)
                        mr = jnp.where(special, br, ar - bi)
                        mi = jnp.where(special, bi, ai + br)
                    else:
                        pr, pi, mr, mi = ar + bi, ai - br, ar - bi, ai + br
                    at_b = side * NB + i * 16 + b
                    planes[at_b, 0] = pr
                    planes[at_b, 1] = pi
                    planes[at_b, 2] = pr * pr + pi * pi
                    planes[at_b, 3] = mr
                    planes[at_b, 4] = mi
                    planes[at_b, 5] = mr * mr + mi * mi
                    return carry

                return lax.fori_loop(0, 16, split, carry, unroll=2)

            lax.fori_loop(0, 2, transform, 0)

        if n == 0:
            idx_cp.wait()

        def gather(q, carry):
            members = [jnp.clip(idx_ref[q, s], 0, 2 * NB) for s in range(4)]
            qx, qy, qg = q // 16, lax.rem(q // 4, 4), lax.rem(q, 4)
            for plane in range(6):
                total = planes[members[0], plane] + planes[members[1], plane]
                total += planes[members[2], plane] + planes[members[3], plane]
                total = total.astype(BF)
                if plane < 3:
                    send1[0, n, qx, qy * 4 + qg, plane] = total
                else:
                    send1[1, n, qy, qx * 4 + qg, plane - 3] = total
            return carry

        lax.fori_loop(0, 64, gather, 0, unroll=4)
        for kind in (0, 1):
            for half in range(2):
                for way in range(2):
                    first(half, n, kind, way).start()
        if n == 0:
            late_tables()
        if n > 0:
            enhance(n - 1)
    enhance(NC - 1)

    for n in range(NC):
        for half in range(2):
            for kind in (1, 2):
                for way in range(2):
                    first(half, n, kind, way).wait_recv()

            def combine(i, carry):
                total = send1[half, n, mine1(half), i].astype(F32)
                total += recv1[half, n, 0, i].astype(F32)
                total += recv1[half, n, 1, i].astype(F32)
                send2[half, n, i // 4, lax.rem(i, 4)] = total.astype(BF)
                return carry

            lax.fori_loop(0, 16, combine, 0, unroll=2)
            for d in (2, 1, 3):
                second(half, n, d).start()

    for n in range(NC):
        for half in range(2):
            for d in (1, 2, 3):
                second(half, n, d).wait_recv()
            def finish(g, carry):
                total = send2[half, n, mine2(half), g].astype(F32)
                for d in (1, 2, 3):
                    total += recv2[half, n, d - 1, g].astype(F32)
                at_rows = pl.ds(pl.multiple_of(half * 64 + g * 16, 16), 16)
                power[at_rows, :] = total[0] * total[0] + total[1] * total[1] - total[2]
                return carry

            lax.fori_loop(0, 4, finish, 0)

        def binned_by(table, value):
            high = value.astype(BF)
            low = (value - high.astype(F32)).astype(BF)
            return dot(table, high) + dot(table, low)

        binned = binned_by(bins_ref[...], power[...])
        zsend[:, :, pl.ds(n * 128, 128)] = binned.reshape(16, 8, 128)

    me = z * 2 + c
    spread = []
    for i, (d, e) in enumerate(z_offsets):
        dest = lax.rem(z + d, 8) * 2 + lax.rem(c + e, 2)
        cp = pltpu.make_async_remote_copy(
            src_ref=zsend.at[dest],
            dst_ref=zrecv.at[c, d],
            send_sem=zs_sem.at[i],
            recv_sem=zr_sem.at[i],
            device_id=z_peer(d, e),
            device_id_type=MESH,
        )
        cp.start()
        spread.append(cp)
    zrecv[c, 0] = zsend[me]
    for cp in spread:
        cp.wait_recv()

    parts = []
    for parity in range(2):
        total = zrecv[parity, 0]
        for d in range(1, 8):
            total += zrecv[parity, d]
        parts.append(total * jnp.concatenate([inv_ref[...]] * NC, axis=1))
    even, odd = parts
    row = lax.broadcasted_iota(jnp.int32, (256, 256), 0)
    col = lax.broadcasted_iota(jnp.int32, (256, 256), 1)
    step = col // 2
    from_even = lax.rem(col, 2) == 0
    up = (row == jnp.where(from_even, step, 128 + step)).astype(BF)
    down = (row == jnp.where(from_even, lax.rem(128 - step, 128), 255 - step)).astype(BF)

    def shuffled(value, perm):
        a = value.astype(BF)
        rest = value - a.astype(F32)
        b = rest.astype(BF)
        cc = (rest - b.astype(F32)).astype(BF)
        out = jnp.dot(a, perm, preferred_element_type=F32)
        out += jnp.dot(b, perm, preferred_element_type=F32)
        return out + jnp.dot(cc, perm, preferred_element_type=F32)

    def cut(value, n):
        return value[:, n * 128 : (n + 1) * 128]

    for n in range(NC):
        plus = shuffled(jnp.concatenate([cut(even, n), cut(odd, n)], axis=1), up)
        even_down = jnp.where(lane == 0, cut(even, (3 - n) % 3), cut(even, 2 - n))
        minus = shuffled(jnp.concatenate([even_down, cut(odd, 2 - n)], axis=1), down)
        for g in range(2):
            out_ref[g, :, pl.ds(n * 256, 256)] = plus[2 * g : 2 * g + 2]
            out_ref[g, :, pl.ds(H + n * 256, 256)] = minus[4 + 2 * g : 6 + 2 * g]

    for cp in exchange + spread:
        cp.wait_send()
    for half in range(2):
        for n in range(NC):
            for d in (1, 2, 3):
                second(half, n, d).wait_send()
            for kind in range(3):
                for way in range(2):
                    first(half, n, kind, way).wait_send()


def on_device(visibility, channel_flags, time_bins, baseline_group_index, owner_map):
    tab = jnp.asarray(tables())
    taper = jnp.asarray(taper_row())
    vmem = pl.BlockSpec(memory_space=pltpu.VMEM)
    anym = pl.BlockSpec(memory_space=pl.ANY)
    dma = pltpu.SemaphoreType.DMA
    return pl.pallas_call(
        kernel,
        out_shape=jax.ShapeDtypeStruct((2, 2, F), F32),
        in_specs=[anym, anym, vmem, vmem, vmem, vmem, vmem],
        out_specs=vmem,
        scratch_shapes=[
            pltpu.VMEM((64, 128), jnp.int32),
            pltpu.SMEM((64, 128), jnp.int32),
            pltpu.VMEM((128, 128), BF),
            pltpu.VMEM((8, 128), F32),
            pltpu.VMEM((NB, 32, F), BF),
            pltpu.VMEM((32, F), F32),
            pltpu.VMEM((2, NB * 32, H), BF),
            pltpu.VMEM((NB * 32, H), BF),
            pltpu.VMEM((H, NC * 256), BF),
            pltpu.VMEM((512, 128), F32),
            pltpu.VMEM((512, 128), F32),
            pltpu.VMEM((2 * NB + 1, 6, 16, 128), F32),
            pltpu.VMEM((2, NC, 4, 16, 3, 16, 128), BF),
            pltpu.VMEM((2, NC, 2, 8, 3, 16, 128), BF),
            pltpu.VMEM((2, NC, 2, 16, 3, 16, 128), BF),
            pltpu.VMEM((2, NC, 4, 4, 3, 16, 128), BF),
            pltpu.VMEM((2, NC, 3, 4, 3, 16, 128), BF),
            pltpu.VMEM((128, 128), F32),
            pltpu.VMEM((16, 8, NC * 128), F32),
            pltpu.VMEM((2, 8, 8, NC * 128), F32),
            dma((PIECES,)),
            dma,
            dma,
            dma((PIECES,)),
            dma((PIECES,)),
            dma((2, NC, 3, 2)),
            dma((2, NC, 3, 2)),
            dma((2, NC, 3)),
            dma((2, NC, 3)),
            dma((15,)),
            dma((15,)),
        ],
        compiler_params=pltpu.CompilerParams(
            collective_id=0, has_side_effects=True, vmem_limit_bytes=56 << 20
        ),
        name="spectra_power",
    )(
        visibility,
        tab,
        channel_flags,
        taper,
        time_bins.reshape(1, 16),
        baseline_group_index.reshape(8, 128),
        owner_map.reshape(1, 64),
    )


def solution(mesh):
    in_specs = (P("bl", "lst", None, None), P("lst", None), P("lst"), P(), P())
    out_specs = P("bl", "lst", None)
    return jax.shard_map(
        on_device, mesh=mesh, in_specs=in_specs, out_specs=out_specs, check_vma=False
    )
```

```python
import functools
import math

import jax
import jax.numpy as jnp
import numpy as np
from jax import lax
from jax.experimental import pallas as pl
from jax.experimental.pallas import tpu as pltpu
from jax.sharding import PartitionSpec as P

MESH = pl.DeviceIdType.MESH
F = 1536
H = F // 2
NC = 3
NB = 32
PIECES = 4
PB = NB // PIECES
BF = jnp.bfloat16
F32 = jnp.float32


def tables():
    f = np.arange(H, dtype=np.int64)[:, None]
    m = np.arange(H // 2, dtype=np.int64)[None, :]
    out = np.zeros((2, H, NC, 2, 128), np.float32)
    for parity in range(2):
        k = 2 * m + parity
        angle = 2.0 * np.pi * ((f * k) % F) / F
        cos, sin = np.cos(angle), np.sin(angle)
        if parity == 0:
            sin[:, 0] = np.cos(np.pi * f[:, 0])
        out[parity, :, :, 0] = (cos / math.sqrt(F)).reshape(H, NC, 128)
        out[parity, :, :, 1] = (sin / math.sqrt(F)).reshape(H, NC, 128)
    return out.reshape(2, H, NC * 256).astype(jnp.bfloat16)


def taper_row():
    phase = np.arange(F, dtype=np.float32) * np.float32(2.0 * math.pi / F)
    phase = phase.astype(np.float64)
    taper = (
        0.35875
        - 0.48829 * np.cos(phase)
        + 0.14128 * np.cos(2.0 * phase)
        - 0.01168 * np.cos(3.0 * phase)
    )
    return taper.astype(np.float32)[None, :]


def kernel(
    vis_ref, tab_hbm, flags_ref, taper_ref, times_ref, group_ref, owner_ref,
    out_ref,
    idx_v, idx_ref, bins_ref, inv_ref,
    xv, w2, yall, ysend, tab, ra, rb, planes, send1, recvf, recv1, send2, recv2,
    power, zsend, zrecv,
    ld_sem, tab_sem, idx_sem, ys_sem, yr_sem, s1_sem, r1_sem, s2_sem, r2_sem,
    zs_sem, zr_sem,
):
    bl = lax.axis_index("bl")
    z = lax.axis_index("lst")
    c = lax.rem(bl, 2)
    y = lax.rem(bl // 2, 4)
    x = bl // 8

    def at(xx, yy, cc, zz):
        return (xx * 8 + yy * 2 + cc, zz)

    def x_peer(d):
        return at(lax.rem(x + d, 4), y, c, z)

    def y_peer(d):
        return at(x, lax.rem(y + d, 4), c, z)

    def z_peer(d, e):
        return at(x, y, lax.rem(c + e, 2), lax.rem(z + d, 8))

    z_offsets = [(d, e) for d in range(8) for e in range(2) if d or e]

    rows = vis_ref.reshape(NB, 32, F)
    loads = []
    for p in range(PIECES):
        cp = pltpu.make_async_copy(
            rows.at[pl.ds(p * PB, PB)], xv.at[pl.ds(p * PB, PB)], ld_sem.at[p]
        )
        cp.start()
        loads.append(cp)
    tab_cp = pltpu.make_async_copy(tab_hbm.at[c], tab, tab_sem)
    tab_cp.start()

    barrier = pltpu.get_barrier_semaphore()
    peers = [z_peer(d, e) for d, e in z_offsets]
    peers += [x_peer(d) for d in (1, 2, 3)] + [y_peer(d) for d in (1, 2, 3)]
    for peer in peers:
        pl.semaphore_signal(barrier, inc=1, device_id=peer, device_id_type=MESH)

    for t in range(16):
        row = taper_ref[...] * flags_ref[pl.ds(t, 1), :].astype(F32)
        w2[pl.ds(2 * t, 2), :] = jnp.broadcast_to(row, (2, F))
    planes[2 * NB] = jnp.zeros((6, 16, 128), F32)
    sign = (1 - 2 * c).astype(F32)

    pl.semaphore_wait(barrier, len(peers))
    exchange = []
    for p in range(PIECES):
        loads[p].wait()

        def fold(b, carry):
            for j in range(6):
                lo_at, hi_at = pl.ds(j * 128, 128), pl.ds(H + j * 128, 128)
                lo = (xv[b, :, lo_at].astype(F32) * w2[:, lo_at]).astype(BF).astype(F32)
                hi = (xv[b, :, hi_at].astype(F32) * w2[:, hi_at]).astype(BF).astype(F32)
                hi = hi * sign
                at_rows = pl.ds(pl.multiple_of(b * 32, 32), 32)
                yall[0, at_rows, lo_at] = (lo + hi).astype(BF)
                ysend[at_rows, lo_at] = (lo - hi).astype(BF)
            return carry

        lax.fori_loop(p * PB, (p + 1) * PB, fold, 0)
        piece = pl.ds(p * PB * 32, PB * 32)
        cp = pltpu.make_async_remote_copy(
            src_ref=ysend.at[piece],
            dst_ref=yall.at[1, piece],
            send_sem=ys_sem.at[p],
            recv_sem=yr_sem.at[p],
            device_id=z_peer(0, 1),
            device_id_type=MESH,
        )
        cp.start()
        exchange.append(cp)

    def iota(shape, dim):
        return lax.broadcasted_iota(jnp.int32, shape, dim)

    def dot(a, b):
        return jnp.dot(a, b, preferred_element_type=F32)

    def flag(condition):
        return condition.astype(F32).astype(BF)

    chip = bl // 2
    groups = group_ref[pl.ds(chip // 2, 1), :]
    here = iota((64, 128), 1) // 64 == lax.rem(chip, 2)
    group_of = flag((iota((64, 128), 0) == groups) & here)
    row_of = flag(iota((64, 64), 0) == owner_ref[...])
    member = dot(row_of, group_of)
    rank = dot(member.astype(BF), flag(iota((128, 128), 0) < iota((128, 128), 1)))
    place = lax.rem(iota((128, 128), 0) + 32 * c, 64)
    offset = jnp.zeros((64, 128), F32)
    for s in range(4):
        weight = jnp.where(iota((128, 128), 1) == s, 64 - place, 0).astype(F32).astype(BF)
        offset += dot(flag((member > 0.5) & (rank == float(s))), weight)
    idx_v[...] = 64 - offset.astype(jnp.int32)
    idx_cp = pltpu.make_async_copy(idx_v, idx_ref, idx_sem)
    idx_cp.start()

    def late_tables():
        seen = jnp.zeros((64, 128), F32)
        for r in range(8):
            seen += (iota((64, 128), 0) == group_ref[pl.ds(r, 1), :]).astype(F32)
        totals = dot(seen.astype(BF), jnp.ones((128, 128), BF))
        mine8 = 2 * bl + lax.rem(iota((8, 64), 0) // 2, 2)
        count = dot(flag(owner_ref[...] == mine8), totals.astype(BF))
        inv_ref[...] = 1.0 / (count * (count - 1.0))

        times = times_ref[...].astype(F32).astype(BF)
        spread_times = flag(lax.rem(iota((16, 128), 1), 16) == iota((16, 128), 0))
        k_bin = dot(times, spread_times).astype(jnp.int32)
        r, k = iota((128, 128), 0), iota((128, 128), 1)
        bins_ref[...] = flag(
            ((r // 16) * 2 + lax.rem(r, 2) == k_bin)
            & (lax.rem(r // 4, 2) == k // 64)
            & (lax.rem(r // 8, 2) * 2 + lax.rem(r // 2, 2) == lax.rem(k // 16, 4))
        )

    tab_cp.wait()

    def peer1(half, d):
        return x_peer(d) if half == 0 else y_peer(d)

    def peer2(half, d):
        return y_peer(d) if half == 0 else x_peer(d)

    def mine1(half):
        return x if half == 0 else y

    def mine2(half):
        return y if half == 0 else x

    def remote(src, dst, send_sem, recv_sem, device):
        return pltpu.make_async_remote_copy(
            src_ref=src,
            dst_ref=dst,
            send_sem=send_sem,
            recv_sem=recv_sem,
            device_id=device,
            device_id_type=MESH,
        )

    def first(half, n, kind, way):
        d = (1, 3)[way]
        dest = lax.rem(mine1(half) + (2 if kind == 0 else d), 4)
        start = 8 * way if kind != 1 else 8 * (1 - way)
        some = pl.ds(start, 8)
        src = send1.at[half, n, dest, some]
        dst = recvf.at[half, n, way] if kind == 0 else recv1.at[half, n, way, some]
        sems = (s1_sem.at[half, n, kind, way], r1_sem.at[half, n, kind, way])
        return remote(src, dst, *sems, peer1(half, d))

    def second(half, n, d):
        sems = (s2_sem.at[half, n, d - 1], r2_sem.at[half, n, d - 1])
        src = send2.at[half, n, lax.rem(mine2(half) + d, 4)]
        return remote(src, recv2.at[half, n, d - 1], *sems, peer2(half, d))

    def spread(n, i):
        d, e = z_offsets[i]
        src = zsend.at[n, lax.rem(z + d, 8) * 2 + lax.rem(c + e, 2)]
        sems = (zs_sem.at[n, i], zr_sem.at[n, i])
        return remote(src, zrecv.at[n, c, d], *sems, z_peer(d, e))

    def enhance(n):
        for half in range(2):
            for way in range(2):
                first(half, n, 0, way).wait_recv()
                dest = lax.rem(mine1(half) + (1, 3)[way], 4)

                def add(i, carry):
                    at_row = way * 8 + i
                    total = send1[half, n, dest, at_row].astype(F32)
                    total += recvf[half, n, way, i].astype(F32)
                    send1[half, n, dest, at_row] = total.astype(BF)
                    return carry

                lax.fori_loop(0, 8, add, 0, unroll=2)
                first(half, n, 2, way).start()

    lane = lax.broadcasted_iota(jnp.int32, (1, 128), 1)
    for n in range(NC):
        special = (lane + c) == 0
        for side in range(2):
            if side == 1 and n == 0:
                for cp in exchange:
                    cp.wait_recv()

            def transform(i, carry):
                at_rows = pl.ds(pl.multiple_of(i * 512, 512), 512)
                prod = jnp.dot(
                    yall[side, at_rows, :],
                    tab[:, pl.ds(n * 256, 256)],
                    preferred_element_type=F32,
                )
                ra[...] = prod[:, :128]
                rb[...] = prod[:, 128:]

                def split(b, carry):
                    start = b * 32
                    ar = ra[pl.ds(start, 16, stride=2), :]
                    ai = ra[pl.ds(start + 1, 16, stride=2), :]
                    br = rb[pl.ds(start, 16, stride=2), :]
                    bi = rb[pl.ds(start + 1, 16, stride=2), :]
                    if n == 0:
                        zero = jnp.zeros_like(ar)
                        pr = ar + jnp.where(special, zero, bi)
                        pi = ai - jnp.where(special, zero, br)
                        mr = jnp.where(special, br, ar - bi)
                        mi = jnp.where(special, bi, ai + br)
                    else:
                        pr, pi, mr, mi = ar + bi, ai - br, ar - bi, ai + br
                    at_b = side * NB + i * 16 + b
                    planes[at_b, 0] = pr
                    planes[at_b, 1] = pi
                    planes[at_b, 2] = pr * pr + pi * pi
                    planes[at_b, 3] = mr
                    planes[at_b, 4] = mi
                    planes[at_b, 5] = mr * mr + mi * mi
                    return carry

                return lax.fori_loop(0, 16, split, carry, unroll=2)

            lax.fori_loop(0, 2, transform, 0)

        if n == 0:
            idx_cp.wait()

        def gather(q, half, to, at_row):
            members = [jnp.clip(idx_ref[q, s], 0, 2 * NB) for s in range(4)]
            for plane in range(3):
                p = half * 3 + plane
                total = planes[members[0], p] + planes[members[1], p]
                total += planes[members[2], p] + planes[members[3], p]
                send1[half, n, to, at_row, plane] = total.astype(BF)

        def gather_block(half, d):
            to = lax.rem(mine1(half) + d, 4)

            def gather_one(i, carry):
                qx, qy = (to, i // 4) if half == 0 else (i // 4, to)
                gather(qx * 16 + qy * 4 + lax.rem(i, 4), half, to, i)
                return carry

            lax.fori_loop(0, 16, gather_one, 0, unroll=4)

        for half in range(2):
            gather_block(half, 2)
            for way in range(2):
                first(half, n, 0, way).start()
        for half in range(2):
            for way in range(2):
                gather_block(half, (1, 3)[way])
                first(half, n, 1, way).start()
        for half in range(2):
            gather_block(half, 0)
        if n == 0:
            late_tables()
        if n > 0:
            enhance(n - 1)
    enhance(NC - 1)

    for n in range(NC):
        for half in range(2):
            for kind in (1, 2):
                for way in range(2):
                    first(half, n, kind, way).wait_recv()

            def combine(i, carry):
                total = send1[half, n, mine1(half), i].astype(F32)
                total += recv1[half, n, 0, i].astype(F32)
                total += recv1[half, n, 1, i].astype(F32)
                send2[half, n, i // 4, lax.rem(i, 4)] = total.astype(BF)
                return carry

            lax.fori_loop(0, 16, combine, 0, unroll=2)
            for d in (2, 1, 3):
                second(half, n, d).start()

    for n in range(NC):
        for half in range(2):
            for d in (1, 2, 3):
                second(half, n, d).wait_recv()
            def finish(g, carry):
                total = send2[half, n, mine2(half), g].astype(F32)
                for d in (1, 2, 3):
                    total += recv2[half, n, d - 1, g].astype(F32)
                at_rows = pl.ds(pl.multiple_of(half * 64 + g * 16, 16), 16)
                power[at_rows, :] = total[0] * total[0] + total[1] * total[1] - total[2]
                return carry

            lax.fori_loop(0, 4, finish, 0)

        def binned_by(table, value):
            high = value.astype(BF)
            low = (value - high.astype(F32)).astype(BF)
            return dot(table, high) + dot(table, low)

        binned = binned_by(bins_ref[...], power[...])
        zsend[n] = binned.reshape(16, 8, 128)
        zrecv[n, c, 0] = zsend[n, z * 2 + c]
        for i in range(15):
            spread(n, i).start()

    parts = [[], []]
    scale = inv_ref[...]
    for n in range(NC):
        for i in range(15):
            spread(n, i).wait_recv()
        for half in range(2):
            total = zrecv[n, half, 0]
            for d in range(1, 8):
                total += zrecv[n, half, d]
            parts[half].append(total * scale)
    even, odd = parts
    row = lax.broadcasted_iota(jnp.int32, (256, 256), 0)
    col = lax.broadcasted_iota(jnp.int32, (256, 256), 1)
    step = col // 2
    from_even = lax.rem(col, 2) == 0
    up = (row == jnp.where(from_even, step, 128 + step)).astype(BF)
    down = (row == jnp.where(from_even, lax.rem(128 - step, 128), 255 - step)).astype(BF)

    def shuffled(value, perm):
        a = value.astype(BF)
        rest = value - a.astype(F32)
        b = rest.astype(BF)
        cc = (rest - b.astype(F32)).astype(BF)
        out = jnp.dot(a, perm, preferred_element_type=F32)
        out += jnp.dot(b, perm, preferred_element_type=F32)
        return out + jnp.dot(cc, perm, preferred_element_type=F32)

    for n in range(NC):
        plus = shuffled(jnp.concatenate([even[n], odd[n]], axis=1), up)
        even_down = jnp.where(lane == 0, even[(3 - n) % 3], even[2 - n])
        minus = shuffled(jnp.concatenate([even_down, odd[2 - n]], axis=1), down)
        for g in range(2):
            out_ref[g, :, pl.ds(n * 256, 256)] = plus[2 * g : 2 * g + 2]
            out_ref[g, :, pl.ds(H + n * 256, 256)] = minus[4 + 2 * g : 6 + 2 * g]

    for cp in exchange:
        cp.wait_send()
    for n in range(NC):
        for i in range(15):
            spread(n, i).wait_send()
    for half in range(2):
        for n in range(NC):
            for d in (1, 2, 3):
                second(half, n, d).wait_send()
            for kind in range(3):
                for way in range(2):
                    first(half, n, kind, way).wait_send()


def on_device(visibility, channel_flags, time_bins, baseline_group_index, owner_map):
    tab = jnp.asarray(tables())
    taper = jnp.asarray(taper_row())
    vmem = pl.BlockSpec(memory_space=pltpu.VMEM)
    anym = pl.BlockSpec(memory_space=pl.ANY)
    dma = pltpu.SemaphoreType.DMA
    return pl.pallas_call(
        kernel,
        out_shape=jax.ShapeDtypeStruct((2, 2, F), F32),
        in_specs=[anym, anym, vmem, vmem, vmem, vmem, vmem],
        out_specs=vmem,
        scratch_shapes=[
            pltpu.VMEM((64, 128), jnp.int32),
            pltpu.SMEM((64, 128), jnp.int32),
            pltpu.VMEM((128, 128), BF),
            pltpu.VMEM((8, 128), F32),
            pltpu.VMEM((NB, 32, F), BF),
            pltpu.VMEM((32, F), F32),
            pltpu.VMEM((2, NB * 32, H), BF),
            pltpu.VMEM((NB * 32, H), BF),
            pltpu.VMEM((H, NC * 256), BF),
            pltpu.VMEM((512, 128), F32),
            pltpu.VMEM((512, 128), F32),
            pltpu.VMEM((2 * NB + 1, 6, 16, 128), F32),
            pltpu.VMEM((2, NC, 4, 16, 3, 16, 128), BF),
            pltpu.VMEM((2, NC, 2, 8, 3, 16, 128), BF),
            pltpu.VMEM((2, NC, 2, 16, 3, 16, 128), BF),
            pltpu.VMEM((2, NC, 4, 4, 3, 16, 128), BF),
            pltpu.VMEM((2, NC, 3, 4, 3, 16, 128), BF),
            pltpu.VMEM((128, 128), F32),
            pltpu.VMEM((NC, 16, 8, 128), F32),
            pltpu.VMEM((NC, 2, 8, 8, 128), F32),
            dma((PIECES,)),
            dma,
            dma,
            dma((PIECES,)),
            dma((PIECES,)),
            dma((2, NC, 3, 2)),
            dma((2, NC, 3, 2)),
            dma((2, NC, 3)),
            dma((2, NC, 3)),
            dma((NC, 15)),
            dma((NC, 15)),
        ],
        compiler_params=pltpu.CompilerParams(
            collective_id=0, has_side_effects=True, vmem_limit_bytes=56 << 20
        ),
        name="spectra_power",
    )(
        visibility,
        tab,
        channel_flags,
        taper,
        time_bins.reshape(1, 16),
        baseline_group_index.reshape(8, 128),
        owner_map.reshape(1, 64),
    )


def solution(mesh):
    in_specs = (P("bl", "lst", None, None), P("lst", None), P("lst"), P(), P())
    out_specs = P("bl", "lst", None)
    return jax.shard_map(
        on_device, mesh=mesh, in_specs=in_specs, out_specs=out_specs, check_vma=False
    )
```

```python
import functools
import math

import jax
import jax.numpy as jnp
import numpy as np
from jax import lax
from jax.experimental import pallas as pl
from jax.experimental.pallas import tpu as pltpu
from jax.sharding import PartitionSpec as P

MESH = pl.DeviceIdType.MESH
F = 1536
H = F // 2
NC = 3
NB = 32
PIECES = 4
PB = NB // PIECES
BF = jnp.bfloat16
F32 = jnp.float32


def tables():
    f = np.arange(H, dtype=np.int64)[:, None]
    m = np.arange(H // 2, dtype=np.int64)[None, :]
    out = np.zeros((2, H, NC, 2, 128), np.float32)
    for parity in range(2):
        k = 2 * m + parity
        angle = 2.0 * np.pi * ((f * k) % F) / F
        cos, sin = np.cos(angle), np.sin(angle)
        if parity == 0:
            sin[:, 0] = np.cos(np.pi * f[:, 0])
        out[parity, :, :, 0] = (cos / math.sqrt(F)).reshape(H, NC, 128)
        out[parity, :, :, 1] = (sin / math.sqrt(F)).reshape(H, NC, 128)
    return out.reshape(2, H, NC * 256).astype(jnp.bfloat16)


def taper_row():
    phase = np.arange(F, dtype=np.float32) * np.float32(2.0 * math.pi / F)
    phase = phase.astype(np.float64)
    taper = (
        0.35875
        - 0.48829 * np.cos(phase)
        + 0.14128 * np.cos(2.0 * phase)
        - 0.01168 * np.cos(3.0 * phase)
    )
    return taper.astype(np.float32)[None, :]


def kernel(
    vis_ref, tab_hbm, flags_hbm, taper_hbm, times_hbm, group_hbm, owner_hbm,
    out_ref,
    flags_ref, taper_ref, times_ref, group_ref, owner_ref, up_ref, down_ref,
    idx_v, idx_ref, bins_ref, inv_ref,
    xv, w2, yall, ysend, tab, ra, rb, planes, send1, recvf, recv1, send2, recv2,
    power, zsend, zrecv,
    small_sem, ld_sem, tab_sem, idx_sem, ys_sem, yr_sem, s1_sem, r1_sem, s2_sem, r2_sem,
    zs_sem, zr_sem,
):
    bl = lax.axis_index("bl")
    z = lax.axis_index("lst")
    c = lax.rem(bl, 2)
    y = lax.rem(bl // 2, 4)
    x = bl // 8

    def at(xx, yy, cc, zz):
        return (xx * 8 + yy * 2 + cc, zz)

    def x_peer(d):
        return at(lax.rem(x + d, 4), y, c, z)

    def y_peer(d):
        return at(x, lax.rem(y + d, 4), c, z)

    def z_peer(d, e):
        return at(x, y, lax.rem(c + e, 2), lax.rem(z + d, 8))

    z_offsets = [(d, e) for d in range(8) for e in range(2) if d or e]

    pairs = [
        (flags_hbm, flags_ref),
        (taper_hbm, taper_ref),
        (group_hbm, group_ref),
        (owner_hbm, owner_ref),
        (times_hbm, times_ref),
    ]
    small = []
    for i, (src, dst) in enumerate(pairs):
        cp = pltpu.make_async_copy(src, dst, small_sem.at[i])
        cp.start()
        small.append(cp)
    rows = vis_ref.reshape(NB, 32, F)
    loads = []
    for p in range(PIECES):
        cp = pltpu.make_async_copy(
            rows.at[pl.ds(p * PB, PB)], xv.at[pl.ds(p * PB, PB)], ld_sem.at[p]
        )
        cp.start()
        loads.append(cp)
    tab_cp = pltpu.make_async_copy(tab_hbm.at[c], tab, tab_sem)
    tab_cp.start()

    barrier = pltpu.get_barrier_semaphore()
    peers = [z_peer(d, e) for d, e in z_offsets]
    peers += [x_peer(d) for d in (1, 2, 3)] + [y_peer(d) for d in (1, 2, 3)]
    for peer in peers:
        pl.semaphore_signal(barrier, inc=1, device_id=peer, device_id_type=MESH)

    small[0].wait()
    small[1].wait()
    for t in range(16):
        row = taper_ref[...] * flags_ref[pl.ds(t, 1), :].astype(F32)
        w2[pl.ds(2 * t, 2), :] = jnp.broadcast_to(row, (2, F))
    planes[2 * NB] = jnp.zeros((6, 16, 128), F32)
    def iota(shape, dim):
        return lax.broadcasted_iota(jnp.int32, shape, dim)

    def dot(a, b):
        return jnp.dot(a, b, preferred_element_type=F32)

    def flag(condition):
        return condition.astype(F32).astype(BF)

    for cp in small[2:]:
        cp.wait()
    chip = bl // 2
    groups = group_ref[pl.ds(chip // 2, 1), :]
    here = iota((64, 128), 1) // 64 == lax.rem(chip, 2)
    group_of = flag((iota((64, 128), 0) == groups) & here)
    row_of = flag(iota((64, 64), 0) == owner_ref[...])
    member = dot(row_of, group_of)
    rank = dot(member.astype(BF), flag(iota((128, 128), 0) < iota((128, 128), 1)))
    place = lax.rem(iota((128, 128), 0) + 32 * c, 64)
    offset = jnp.zeros((64, 128), F32)
    for s in range(4):
        weight = jnp.where(iota((128, 128), 1) == s, 64 - place, 0).astype(F32).astype(BF)
        offset += dot(flag((member > 0.5) & (rank == float(s))), weight)
    idx_v[...] = 64 - offset.astype(jnp.int32)
    idx_cp = pltpu.make_async_copy(idx_v, idx_ref, idx_sem)
    idx_cp.start()

    sign = (1 - 2 * c).astype(F32)

    pl.semaphore_wait(barrier, len(peers))
    exchange = []
    for p in range(PIECES):
        loads[p].wait()

        def fold(b, carry):
            for j in range(6):
                lo_at, hi_at = pl.ds(j * 128, 128), pl.ds(H + j * 128, 128)
                lo = (xv[b, :, lo_at].astype(F32) * w2[:, lo_at]).astype(BF).astype(F32)
                hi = (xv[b, :, hi_at].astype(F32) * w2[:, hi_at]).astype(BF).astype(F32)
                hi = hi * sign
                at_rows = pl.ds(pl.multiple_of(b * 32, 32), 32)
                yall[0, at_rows, lo_at] = (lo + hi).astype(BF)
                ysend[at_rows, lo_at] = (lo - hi).astype(BF)
            return carry

        lax.fori_loop(p * PB, (p + 1) * PB, fold, 0)
        piece = pl.ds(p * PB * 32, PB * 32)
        cp = pltpu.make_async_remote_copy(
            src_ref=ysend.at[piece],
            dst_ref=yall.at[1, piece],
            send_sem=ys_sem.at[p],
            recv_sem=yr_sem.at[p],
            device_id=z_peer(0, 1),
            device_id_type=MESH,
        )
        cp.start()
        exchange.append(cp)

    def late_tables():
        seen = jnp.zeros((64, 128), F32)
        for r in range(8):
            seen += (iota((64, 128), 0) == group_ref[pl.ds(r, 1), :]).astype(F32)
        totals = dot(seen.astype(BF), jnp.ones((128, 128), BF))
        mine8 = 2 * bl + lax.rem(iota((8, 64), 0) // 2, 2)
        count = dot(flag(owner_ref[...] == mine8), totals.astype(BF))
        inv_ref[...] = 1.0 / (count * (count - 1.0))

        times = times_ref[...].astype(F32).astype(BF)
        spread_times = flag(lax.rem(iota((16, 128), 1), 16) == iota((16, 128), 0))
        k_bin = dot(times, spread_times).astype(jnp.int32)
        r, k = iota((128, 128), 0), iota((128, 128), 1)
        bins_ref[...] = flag(
            ((r // 16) * 2 + lax.rem(r, 2) == k_bin)
            & (lax.rem(r // 4, 2) == k // 64)
            & (lax.rem(r // 8, 2) * 2 + lax.rem(r // 2, 2) == lax.rem(k // 16, 4))
        )

        row, col = iota((256, 256), 0), iota((256, 256), 1)
        step = col // 2
        from_even = lax.rem(col, 2) == 0
        up_ref[...] = flag(row == jnp.where(from_even, step, 128 + step))
        down_ref[...] = flag(
            row == jnp.where(from_even, lax.rem(128 - step, 128), 255 - step)
        )

    tab_cp.wait()

    def peer1(half, d):
        return x_peer(d) if half == 0 else y_peer(d)

    def peer2(half, d):
        return y_peer(d) if half == 0 else x_peer(d)

    def mine1(half):
        return x if half == 0 else y

    def mine2(half):
        return y if half == 0 else x

    def remote(src, dst, send_sem, recv_sem, device):
        return pltpu.make_async_remote_copy(
            src_ref=src,
            dst_ref=dst,
            send_sem=send_sem,
            recv_sem=recv_sem,
            device_id=device,
            device_id_type=MESH,
        )

    def first(half, n, kind, way):
        d = (1, 3)[way]
        dest = lax.rem(mine1(half) + (2 if kind == 0 else d), 4)
        start = 8 * way if kind != 1 else 8 * (1 - way)
        some = pl.ds(start, 8)
        src = send1.at[half, n, dest, some]
        dst = recvf.at[half, n, way] if kind == 0 else recv1.at[half, n, way, some]
        sems = (s1_sem.at[half, n, kind, way], r1_sem.at[half, n, kind, way])
        return remote(src, dst, *sems, peer1(half, d))

    def second(half, n, d):
        sems = (s2_sem.at[half, n, d - 1], r2_sem.at[half, n, d - 1])
        src = send2.at[half, n, lax.rem(mine2(half) + d, 4)]
        return remote(src, recv2.at[half, n, d - 1], *sems, peer2(half, d))

    def spread(n, i):
        d, e = z_offsets[i]
        src = zsend.at[n, lax.rem(z + d, 8) * 2 + lax.rem(c + e, 2)]
        sems = (zs_sem.at[n, i], zr_sem.at[n, i])
        return remote(src, zrecv.at[n, c, d], *sems, z_peer(d, e))

    def enhance(n):
        for half in range(2):
            for way in range(2):
                first(half, n, 0, way).wait_recv()
                dest = lax.rem(mine1(half) + (1, 3)[way], 4)

                def add(i, carry):
                    at_row = way * 8 + i
                    total = send1[half, n, dest, at_row].astype(F32)
                    total += recvf[half, n, way, i].astype(F32)
                    send1[half, n, dest, at_row] = total.astype(BF)
                    return carry

                lax.fori_loop(0, 8, add, 0, unroll=8)
                first(half, n, 2, way).start()

    lane = lax.broadcasted_iota(jnp.int32, (1, 128), 1)
    for n in range(NC):
        special = (lane + c) == 0
        for side in range(2):
            if side == 1 and n == 0:
                for cp in exchange:
                    cp.wait_recv()

            def transform(i, carry):
                at_rows = pl.ds(pl.multiple_of(i * 512, 512), 512)
                prod = jnp.dot(
                    yall[side, at_rows, :],
                    tab[:, pl.ds(n * 256, 256)],
                    preferred_element_type=F32,
                )
                ra[...] = prod[:, :128]
                rb[...] = prod[:, 128:]

                def split(b, carry):
                    start = b * 32
                    ar = ra[pl.ds(start, 16, stride=2), :]
                    ai = ra[pl.ds(start + 1, 16, stride=2), :]
                    br = rb[pl.ds(start, 16, stride=2), :]
                    bi = rb[pl.ds(start + 1, 16, stride=2), :]
                    if n == 0:
                        zero = jnp.zeros_like(ar)
                        pr = ar + jnp.where(special, zero, bi)
                        pi = ai - jnp.where(special, zero, br)
                        mr = jnp.where(special, br, ar - bi)
                        mi = jnp.where(special, bi, ai + br)
                    else:
                        pr, pi, mr, mi = ar + bi, ai - br, ar - bi, ai + br
                    at_b = side * NB + i * 16 + b
                    planes[at_b, 0] = pr
                    planes[at_b, 1] = pi
                    planes[at_b, 2] = pr * pr + pi * pi
                    planes[at_b, 3] = mr
                    planes[at_b, 4] = mi
                    planes[at_b, 5] = mr * mr + mi * mi
                    return carry

                return lax.fori_loop(0, 16, split, carry, unroll=2)

            lax.fori_loop(0, 2, transform, 0)

        if n == 0:
            idx_cp.wait()

        def gather(q, half, to, at_row):
            members = [jnp.clip(idx_ref[q, s], 0, 2 * NB) for s in range(4)]
            for plane in range(3):
                p = half * 3 + plane
                total = planes[members[0], p] + planes[members[1], p]
                total += planes[members[2], p] + planes[members[3], p]
                send1[half, n, to, at_row, plane] = total.astype(BF)

        def gather_block(half, d):
            to = lax.rem(mine1(half) + d, 4)

            def gather_one(i, carry):
                qx, qy = (to, i // 4) if half == 0 else (i // 4, to)
                gather(qx * 16 + qy * 4 + lax.rem(i, 4), half, to, i)
                return carry

            lax.fori_loop(0, 16, gather_one, 0, unroll=16)

        for half in range(2):
            gather_block(half, 2)
            for way in range(2):
                first(half, n, 0, way).start()
        for half in range(2):
            for way in range(2):
                gather_block(half, (1, 3)[way])
                first(half, n, 1, way).start()
        for half in range(2):
            gather_block(half, 0)
        if n == 0:
            late_tables()
        if n > 0:
            enhance(n - 1)
    enhance(NC - 1)

    for n in range(NC):
        for half in range(2):
            for kind in (1, 2):
                for way in range(2):
                    first(half, n, kind, way).wait_recv()

            def combine(i, carry):
                total = send1[half, n, mine1(half), i].astype(F32)
                total += recv1[half, n, 0, i].astype(F32)
                total += recv1[half, n, 1, i].astype(F32)
                send2[half, n, i // 4, lax.rem(i, 4)] = total.astype(BF)
                return carry

            lax.fori_loop(0, 16, combine, 0, unroll=4)
            for d in (2, 1, 3):
                second(half, n, d).start()

    for n in range(NC):
        for half in range(2):
            for d in (1, 2, 3):
                second(half, n, d).wait_recv()
            def finish(g, carry):
                total = send2[half, n, mine2(half), g].astype(F32)
                for d in (1, 2, 3):
                    total += recv2[half, n, d - 1, g].astype(F32)
                at_rows = pl.ds(pl.multiple_of(half * 64 + g * 16, 16), 16)
                power[at_rows, :] = total[0] * total[0] + total[1] * total[1] - total[2]
                return carry

            lax.fori_loop(0, 4, finish, 0)

        def binned_by(table, value):
            high = value.astype(BF)
            low = (value - high.astype(F32)).astype(BF)
            return dot(table, high) + dot(table, low)

        binned = binned_by(bins_ref[...], power[...])
        zsend[n] = binned.reshape(16, 8, 128)
        zrecv[n, c, 0] = zsend[n, z * 2 + c]
        for i in range(15):
            spread(n, i).start()

    parts = [[], []]
    scale = inv_ref[...]
    for n in range(NC):
        for i in range(15):
            spread(n, i).wait_recv()
        for half in range(2):
            total = zrecv[n, half, 0]
            for d in range(1, 8):
                total += zrecv[n, half, d]
            parts[half].append(total * scale)
    even, odd = parts
    up, down = up_ref[...], down_ref[...]

    def shuffled(value, perm):
        a = value.astype(BF)
        rest = value - a.astype(F32)
        b = rest.astype(BF)
        cc = (rest - b.astype(F32)).astype(BF)
        out = jnp.dot(a, perm, preferred_element_type=F32)
        out += jnp.dot(b, perm, preferred_element_type=F32)
        return out + jnp.dot(cc, perm, preferred_element_type=F32)

    for n in range(NC):
        plus = shuffled(jnp.concatenate([even[n], odd[n]], axis=1), up)
        even_down = jnp.where(lane == 0, even[(3 - n) % 3], even[2 - n])
        minus = shuffled(jnp.concatenate([even_down, odd[2 - n]], axis=1), down)
        for g in range(2):
            out_ref[g, :, pl.ds(n * 256, 256)] = plus[2 * g : 2 * g + 2]
            out_ref[g, :, pl.ds(H + n * 256, 256)] = minus[4 + 2 * g : 6 + 2 * g]

    for cp in exchange:
        cp.wait_send()
    for n in range(NC):
        for i in range(15):
            spread(n, i).wait_send()
    for half in range(2):
        for n in range(NC):
            for d in (1, 2, 3):
                second(half, n, d).wait_send()
            for kind in range(3):
                for way in range(2):
                    first(half, n, kind, way).wait_send()


def on_device(visibility, channel_flags, time_bins, baseline_group_index, owner_map):
    tab = jnp.asarray(tables())
    taper = jnp.asarray(taper_row())
    vmem = pl.BlockSpec(memory_space=pltpu.VMEM)
    anym = pl.BlockSpec(memory_space=pl.ANY)
    dma = pltpu.SemaphoreType.DMA
    return pl.pallas_call(
        kernel,
        out_shape=jax.ShapeDtypeStruct((2, 2, F), F32),
        in_specs=[anym] * 7,
        out_specs=vmem,
        scratch_shapes=[
            pltpu.VMEM((16, F), jnp.int32),
            pltpu.VMEM((1, F), F32),
            pltpu.VMEM((1, 16), jnp.int32),
            pltpu.VMEM((8, 128), jnp.int32),
            pltpu.VMEM((1, 64), jnp.int32),
            pltpu.VMEM((256, 256), BF),
            pltpu.VMEM((256, 256), BF),
            pltpu.VMEM((64, 128), jnp.int32),
            pltpu.SMEM((64, 128), jnp.int32),
            pltpu.VMEM((128, 128), BF),
            pltpu.VMEM((8, 128), F32),
            pltpu.VMEM((NB, 32, F), BF),
            pltpu.VMEM((32, F), F32),
            pltpu.VMEM((2, NB * 32, H), BF),
            pltpu.VMEM((NB * 32, H), BF),
            pltpu.VMEM((H, NC * 256), BF),
            pltpu.VMEM((512, 128), F32),
            pltpu.VMEM((512, 128), F32),
            pltpu.VMEM((2 * NB + 1, 6, 16, 128), F32),
            pltpu.VMEM((2, NC, 4, 16, 3, 16, 128), BF),
            pltpu.VMEM((2, NC, 2, 8, 3, 16, 128), BF),
            pltpu.VMEM((2, NC, 2, 16, 3, 16, 128), BF),
            pltpu.VMEM((2, NC, 4, 4, 3, 16, 128), BF),
            pltpu.VMEM((2, NC, 3, 4, 3, 16, 128), BF),
            pltpu.VMEM((128, 128), F32),
            pltpu.VMEM((NC, 16, 8, 128), F32),
            pltpu.VMEM((NC, 2, 8, 8, 128), F32),
            dma((5,)),
            dma((PIECES,)),
            dma,
            dma,
            dma((PIECES,)),
            dma((PIECES,)),
            dma((2, NC, 3, 2)),
            dma((2, NC, 3, 2)),
            dma((2, NC, 3)),
            dma((2, NC, 3)),
            dma((NC, 15)),
            dma((NC, 15)),
        ],
        compiler_params=pltpu.CompilerParams(
            collective_id=0, has_side_effects=True, vmem_limit_bytes=56 << 20
        ),
        name="spectra_power",
    )(
        visibility,
        tab,
        channel_flags,
        taper,
        time_bins.reshape(1, 16),
        baseline_group_index.reshape(8, 128),
        owner_map.reshape(1, 64),
    )


def solution(mesh):
    in_specs = (P("bl", "lst", None, None), P("lst", None), P("lst"), P(), P())
    out_specs = P("bl", "lst", None)
    return jax.shard_map(
        on_device, mesh=mesh, in_specs=in_specs, out_specs=out_specs, check_vma=False
    )
```
